32 devices in a mesh: groups: 2 (over x), ctx: 16 (over z, y, core).
Axes of the slice: x: 2, y: 2, z: 4, core: 2. Of those that a mesh axis runs over, the one named last changes fastest.
Arguments:
- queries: bfloat16 [256, 8192], P(('groups', 'ctx')), parts along dimension 0, may hold values from -8 to 8
- prefix_key_heads: bfloat16 [16384, 1024], P(('groups', 'ctx')), parts along dimension 0, may hold values from -8 to 8
- prefix_value_heads: bfloat16 [16384, 1024], P(('groups', 'ctx')), parts along dimension 0, may hold values from -6 to 6
- tree_key_heads: bfloat16 [256, 1024], P(('groups', 'ctx')), parts along dimension 0, may hold values from -16 to 16
- tree_value_heads: bfloat16 [256, 1024], P(('groups', 'ctx')), parts along dimension 0, may hold values from -6 to 6
- token_embed: bfloat16 [256, 8192], P(('groups', 'ctx')), parts along dimension 0, may hold values from -12 to 12
- fc_embed: bfloat16 [8192, 8192], P('ctx'), may hold values from -0.25 to 0.25
- fc_feature: bfloat16 [8192, 8192], P('ctx'), may hold values from -0.0625 to 0.0625
- draft_gain: float32 [8192], replicated, may hold values from 0.5 to 1.5
- parents: int32 [4, 64], P('groups'), parts along dimension 0, may hold values from 0 to 62, as said below
- accepted: int32 [4], P('groups'), parts along dimension 0, may hold values from 0 to 63, as said below
Outputs:
- attended: bfloat16 [256, 8192], P(('groups', 'ctx')), parts along dimension 0
- draft_input: bfloat16 [256, 8192], P(('groups', 'ctx')), parts along dimension 0
The draws below stay inside these ranges and needn't reach their ends.
There are 2 independent parts, one for each index of `groups`. The reference program is written for one: setup_inputs(seed, part) draws one part's arguments, and reference() takes and returns one part's arrays. A program takes and returns all parts, laid end to end along the dimension named above; an argument that names none is the same for every part. Nothing has to cross between parts.
Inputs may be any that keep to these rules, and one draw needn't show every extreme that they name: parents[t, 0] = 0 marks the root; every other node's parent is an earlier node of the same tree; no node lies more than 6 steps below its root, and every tree has a node exactly 6 steps below it. The accepted rows of tree t are node accepted[t] and all its ancestors, so at most 7 rows a tree; in every draw some tree accepts exactly 7 rows.
All inputs are finite; a program needn't handle non-finite values.
Results may differ from the reference program's by a relative error of at most 0.0028.
Values may be sent and summed in bfloat16 or wider, within the bound.
A program may use at most 128 MiB of HBM per device.

```python
import jax
import jax.numpy as jnp
from jax import lax

D = 8192
QUERY_HEADS = 64
KEY_HEADS = 8
HEAD_WIDTH = 128
TREE_NODES = 64
ACC = 7
DRAFT_TREES = 2
PREFIX_PER_SHARD = 512
TREE_ROW_TOTAL = 128
PREFIX_LENGTH = 8192
N_CTX = 16


def query_block(key):
    base_key = jax.random.fold_in(key, 11)
    key_scale, key_value_pair = jax.random.split(base_key)
    row_scaling = jnp.exp(jax.random.uniform(key_scale, (TREE_ROW_TOTAL, 1, 1), minval=jnp.log(0.4), maxval=jnp.log(4.0)))
    value_rows = jax.random.normal(key_value_pair, (TREE_ROW_TOTAL, QUERY_HEADS, HEAD_WIDTH))
    queries = jnp.clip(value_rows * row_scaling, -8.0, 8.0)
    return (queries, row_scaling)


def draw_queries(key, part):
    queries, row_scaling = query_block(key)
    return queries.reshape(TREE_ROW_TOTAL, QUERY_HEADS * HEAD_WIDTH).astype(jnp.bfloat16)


def draw_tree_key_heads(key, part):
    queries, row_scaling = query_block(key)
    queries_per_group = QUERY_HEADS // KEY_HEADS
    grouped_heads = jnp.sum(queries.reshape(TREE_ROW_TOTAL, KEY_HEADS, queries_per_group, HEAD_WIDTH), axis=2) / row_scaling
    jitter_portion = jax.random.normal(jax.random.fold_in(key, 12), (TREE_ROW_TOTAL, KEY_HEADS, HEAD_WIDTH))
    tree_key_rows = 2.5 * grouped_heads / jnp.sqrt(1.0 * queries_per_group) + 0.5 * jitter_portion
    return jnp.clip(tree_key_rows, -16.0, 16.0).reshape(TREE_ROW_TOTAL, KEY_HEADS * HEAD_WIDTH).astype(jnp.bfloat16)


def draw_prefix_key_heads(key, part):
    base_key = jax.random.fold_in(key, 21)
    key_scale, key_value_pair = jax.random.split(base_key)
    position_scale = jnp.exp(jax.random.uniform(key_scale, (PREFIX_LENGTH, 1, 1), minval=jnp.log(0.25), maxval=jnp.log(2.5)))
    value_rows = jax.random.normal(key_value_pair, (PREFIX_LENGTH, KEY_HEADS, HEAD_WIDTH))
    prefix_key_rows = jnp.clip(value_rows * position_scale, -8.0, 8.0)
    return prefix_key_rows.reshape(PREFIX_LENGTH, KEY_HEADS * HEAD_WIDTH).astype(jnp.bfloat16)


def draw_prefix_value_heads(key, part):
    base_key = jax.random.fold_in(key, 31)
    key_averages, key_jitter = jax.random.split(base_key)
    region_averages = jax.random.normal(key_averages, (8, KEY_HEADS * HEAD_WIDTH))
    region_of = jnp.arange(PREFIX_LENGTH, dtype=jnp.int32) * 8 // PREFIX_LENGTH
    jitter_portion = 0.7 * jax.random.normal(key_jitter, (PREFIX_LENGTH, KEY_HEADS * HEAD_WIDTH))
    return jnp.clip(region_averages[region_of] + jitter_portion, -6.0, 6.0).astype(jnp.bfloat16)


def draw_token_embed(key, part):
    base_key = jax.random.fold_in(key, 41)
    key_scale, key_value_pair = jax.random.split(base_key, 2)
    row_scaling = jnp.exp(jax.random.uniform(key_scale, (TREE_ROW_TOTAL, 1), minval=jnp.log(0.3), maxval=jnp.log(3.0)))
    value_rows = jax.random.normal(key_value_pair, (TREE_ROW_TOTAL, D))
    return jnp.clip(value_rows * row_scaling, -12.0, 12.0).astype(jnp.bfloat16)


def draw_fc_embed(key, part):
    base_key = jax.random.fold_in(key, 51)
    key_scale, key_value_pair = jax.random.split(base_key)
    column_scale = jnp.exp(jax.random.uniform(key_scale, (1, D), minval=jnp.log(0.3), maxval=jnp.log(3.0)))
    value_rows = jax.random.normal(key_value_pair, (D, D))
    return jnp.clip(value_rows * column_scale / jnp.sqrt(1.0 * D), -0.25, 0.25).astype(jnp.bfloat16)


def tree_shapes(key):
    base_key = jax.random.fold_in(key, 61)
    tree_keys_all = jax.random.split(base_key, DRAFT_TREES)

    def one_tree(tree_key):
        key_chain, key_pick = jax.random.split(tree_key)
        shuffled = jax.random.permutation(key_chain, TREE_NODES - 1).astype(jnp.int32) + 1
        chain_nodes = jnp.sort(shuffled[:ACC - 1])
        chain_prev = jnp.concatenate([jnp.zeros((1,), jnp.int32), chain_nodes[:-1]])
        on_chain = (jnp.arange(TREE_NODES, dtype=jnp.int32)[:, None] == chain_nodes[None, :]).astype(jnp.int32)
        chain_parent = jnp.sum(on_chain * chain_prev[None, :], axis=1)
        is_chain = jnp.sum(on_chain, axis=1) > 0
        ranking = jax.random.randint(key_pick, (TREE_NODES, TREE_NODES), 0, 1 << 20) * TREE_NODES + jnp.arange(TREE_NODES, dtype=jnp.int32)[None, :]

        def attach(depth_now, node_index):
            eligible = (jnp.arange(TREE_NODES, dtype=jnp.int32) < node_index) & (depth_now < ACC - 1)
            picked = jnp.argmax(jnp.where(eligible, ranking[node_index], -1)).astype(jnp.int32)
            parent = jnp.where(is_chain[node_index], chain_parent[node_index], picked)
            depth_now = depth_now.at[node_index].set(depth_now[parent] + 1)
            return (depth_now, parent)
        depth_start = jnp.zeros((TREE_NODES,), jnp.int32)
        depth_end, later_parents = lax.scan(attach, depth_start, jnp.arange(1, TREE_NODES, dtype=jnp.int32))
        tree_parents = jnp.concatenate([jnp.zeros((1,), jnp.int32), later_parents])
        return (tree_parents, chain_nodes[ACC - 2])
    return jax.vmap(one_tree)(tree_keys_all)


def draw_parents(key, part):
    tree_parents, chain_end = tree_shapes(key)
    return tree_parents.astype(jnp.int32)


def draw_accepted(key, part):
    tree_parents, chain_end = tree_shapes(key)
    base_key = jax.random.fold_in(key, 71)
    key_nodes, key_full = jax.random.split(base_key)
    random_nodes = jax.random.randint(key_nodes, (DRAFT_TREES,), 0, TREE_NODES)
    full_tree = jax.random.randint(key_full, (), 0, DRAFT_TREES)
    return jnp.where(jnp.arange(DRAFT_TREES, dtype=jnp.int32) == full_tree, chain_end, random_nodes).astype(jnp.int32)


def levels(key, extent, cuts, least, largest):
    loudness = 1.0
    for position, shards_of in cuts:
        heights = jax.random.uniform(jax.random.fold_in(jax.random.fold_in(key, 6), position), (shards_of,), jnp.float32, least / len(cuts), largest / len(cuts))
        loudness = loudness * jnp.repeat(jnp.exp(heights), extent[position] // shards_of).reshape((-1,) + (1,) * (len(extent) - 1 - position))
    return loudness


def scatter_about(rng, dims, scale, limit, pieces=(), kind=jnp.bfloat16):
    loudness = levels(rng, dims, pieces, -0.22, 0.18) if pieces else 1.0
    drawn = jax.random.normal(rng, dims, jnp.float32) * scale * loudness
    return jnp.minimum(jnp.maximum(drawn, -limit), limit).astype(kind)


def setup_inputs(seed: int = 0, part: int = 0) -> dict:
    keys = jax.random.split(jax.random.key(seed), 12)
    own_keys = jax.random.split(jax.random.fold_in(keys[11], part), 12)
    return {
        "queries": draw_queries(jax.random.fold_in(jax.random.fold_in(keys[11], part), 71), part),
        "prefix_key_heads": draw_prefix_key_heads(jax.random.fold_in(jax.random.fold_in(keys[11], part), 71), part),
        "prefix_value_heads": draw_prefix_value_heads(jax.random.fold_in(jax.random.fold_in(keys[11], part), 71), part),
        "tree_key_heads": draw_tree_key_heads(jax.random.fold_in(jax.random.fold_in(keys[11], part), 71), part),
        "tree_value_heads": scatter_about(own_keys[4], (TREE_ROW_TOTAL, KEY_HEADS * HEAD_WIDTH), 1.0, 6.0, ((0, 16),)),
        "token_embed": draw_token_embed(jax.random.fold_in(jax.random.fold_in(keys[11], part), 71), part),
        "fc_embed": draw_fc_embed(jax.random.fold_in(keys[11], 71), part),
        "fc_feature": scatter_about(keys[7], (D, D), D ** -0.5, 0.0625, ((0, 16),)),
        "draft_gain": jnp.clip(1.0 + 0.1 * jax.random.normal(keys[8], (D,), jnp.float32), 0.5, 1.5),
        "parents": draw_parents(jax.random.fold_in(jax.random.fold_in(keys[11], part), 71), part),
        "accepted": draw_accepted(jax.random.fold_in(jax.random.fold_in(keys[11], part), 71), part),
    }


highest = lax.Precision.HIGHEST
negative_fill = -1e+30

def ancestors(parents):
    nodes = parents.shape[1]
    column = jnp.arange(nodes, dtype=jnp.int32)
    upward = (parents[:, :, None] == column[None, None, :]).astype(jnp.float32)
    closure = jnp.maximum(upward, jnp.eye(nodes, dtype=jnp.float32)[None])
    for repeat in range(max(1, (nodes - 1).bit_length())):
        closure = jnp.minimum(jnp.einsum('tij,tjk->tik', closure, closure, precision=highest), 1.0)
    return closure

def path_rows(closure, accepted):
    nodes = closure.shape[1]
    chosen = (accepted[:, None] == jnp.arange(nodes, dtype=jnp.int32)[None, :]).astype(jnp.float32)
    return jnp.einsum('ti,tij->tj', chosen, closure, precision=highest)

def reference(queries, prefix_key_heads, prefix_value_heads, tree_key_heads, tree_value_heads, token_embed, fc_embed, fc_feature, draft_gain, parents, accepted):
    every_row = DRAFT_TREES * TREE_NODES
    queries_per_group = QUERY_HEADS // KEY_HEADS
    scale_factor = HEAD_WIDTH ** (-0.5)
    grouped_query = queries.astype(jnp.float32).reshape(every_row, KEY_HEADS, queries_per_group, HEAD_WIDTH)

    def block_step(carry, block_index):
        run_max, run_num, run_den = carry
        leading_rows = (block_index * PREFIX_PER_SHARD).astype(jnp.int32)
        key_block_slice = lax.dynamic_slice_in_dim(prefix_key_heads, leading_rows, PREFIX_PER_SHARD, 0).astype(jnp.float32).reshape(PREFIX_PER_SHARD, KEY_HEADS, HEAD_WIDTH)
        value_block_slice = lax.dynamic_slice_in_dim(prefix_value_heads, leading_rows, PREFIX_PER_SHARD, 0).astype(jnp.float32).reshape(PREFIX_PER_SHARD, KEY_HEADS, HEAD_WIDTH)
        scores = jnp.einsum('rgid,kgd->rgik', grouped_query, key_block_slice, precision=highest) * scale_factor
        block_max = lax.optimization_barrier(jnp.max(scores, axis=3))
        weights = jnp.exp(scores - block_max[..., None])
        block_den = lax.optimization_barrier(jnp.sum(weights, axis=3))
        rounded = lax.optimization_barrier(weights.astype(jnp.bfloat16)).astype(jnp.float32)
        block_num = jnp.einsum('rgik,kgd->rgid', rounded, value_block_slice, precision=highest)
        new_max = jnp.maximum(run_max, block_max)
        old_factor = jnp.exp(run_max - new_max)
        new_factor = jnp.exp(block_max - new_max)
        run_num = run_num * old_factor[..., None] + block_num * new_factor[..., None]
        run_den = run_den * old_factor + block_den * new_factor
        return ((new_max, run_num, run_den), None)
    initial_maximum = jnp.full((every_row, KEY_HEADS, queries_per_group), negative_fill, jnp.float32)
    initial_numerator = jnp.zeros((every_row, KEY_HEADS, queries_per_group, HEAD_WIDTH), jnp.float32)
    initial_denominator = jnp.zeros((every_row, KEY_HEADS, queries_per_group), jnp.float32)
    (pref_max, pref_num, pref_den), unused = lax.scan(block_step, (initial_maximum, initial_numerator, initial_denominator), jnp.arange(N_CTX, dtype=jnp.int32))
    closure = ancestors(parents)
    tree_query = grouped_query.reshape(DRAFT_TREES, TREE_NODES, KEY_HEADS, queries_per_group, HEAD_WIDTH)
    tree_key_rows = tree_key_heads.astype(jnp.float32).reshape(DRAFT_TREES, TREE_NODES, KEY_HEADS, HEAD_WIDTH)
    tree_value_rows = tree_value_heads.astype(jnp.float32).reshape(DRAFT_TREES, TREE_NODES, KEY_HEADS, HEAD_WIDTH)
    tree_scores = jnp.einsum('tngid,tjgd->tngij', tree_query, tree_key_rows, precision=highest) * scale_factor
    tree_scores = jnp.where(closure[:, :, None, None, :] > 0.5, tree_scores, negative_fill)
    tree_maximum = lax.optimization_barrier(jnp.max(tree_scores, axis=4))
    tree_weights = jnp.exp(tree_scores - tree_maximum[..., None])
    tree_denominator = lax.optimization_barrier(jnp.sum(tree_weights, axis=4))
    rounded_tree = lax.optimization_barrier(tree_weights.astype(jnp.bfloat16)).astype(jnp.float32)
    tree_numerator = jnp.einsum('tngij,tjgd->tngid', rounded_tree, tree_value_rows, precision=highest)
    tree_maximum = tree_maximum.reshape(every_row, KEY_HEADS, queries_per_group)
    tree_denominator = tree_denominator.reshape(every_row, KEY_HEADS, queries_per_group)
    tree_numerator = tree_numerator.reshape(every_row, KEY_HEADS, queries_per_group, HEAD_WIDTH)
    final_max = jnp.maximum(pref_max, tree_maximum)
    pref_scale = jnp.exp(pref_max - final_max)
    tree_scale = jnp.exp(tree_maximum - final_max)
    numer = pref_num * pref_scale[..., None] + tree_numerator * tree_scale[..., None]
    denom = pref_den * pref_scale + tree_denominator * tree_scale
    attended = (numer / denom[..., None]).reshape(every_row, QUERY_HEADS * HEAD_WIDTH).astype(jnp.bfloat16)
    joined = jnp.dot(token_embed, fc_embed, preferred_element_type=jnp.float32) + jnp.dot(attended, fc_feature, preferred_element_type=jnp.float32)
    mean_square = lax.optimization_barrier(jnp.mean(joined * joined, axis=1, keepdims=True))
    normed = joined * lax.rsqrt(mean_square + 1e-06) * draft_gain[None, :]
    on_path = path_rows(closure, accepted).reshape(every_row, 1)
    draft_input = jnp.where(on_path > 0.5, normed, 0.0).astype(jnp.bfloat16)
    return (attended, draft_input)
```

```python
import functools

import jax
import jax.numpy as jnp
from jax import lax
from jax.experimental import pallas as pl
from jax.experimental.pallas import tpu as pltpu
from jax.sharding import PartitionSpec as P

QUERY_HEADS = 64
KEY_HEADS = 8
HEAD_WIDTH = 128
GROUP = QUERY_HEADS // KEY_HEADS
PATH_ROWS = 7
negative_fill = -1e30


def round_up(value, step):
    return (value + step - 1) // step * step


def ancestors(parents):
    nodes = parents.shape[1]
    column = jnp.arange(nodes, dtype=jnp.int32)
    upward = parents[:, :, None] == column[None, None, :]
    closure = (upward | jnp.eye(nodes, dtype=bool)[None]).astype(jnp.bfloat16)
    for repeat in range((PATH_ROWS - 1).bit_length()):
        counts = jnp.einsum("tij,tjk->tik", closure, closure, preferred_element_type=jnp.float32)
        closure = jnp.minimum(counts, 1.0).astype(jnp.bfloat16)
    return closure


def attention_kernel(block, q_ref, k_ref, v_ref, tk_ref, tv_ref, mask_ref, num_ref, stat_ref):
    scale_factor = HEAD_WIDTH ** (-0.5)
    query_rows = q_ref.shape[0]
    tile = min(256, query_rows)
    blocks = k_ref.shape[0] // block

    @pl.loop(0, query_rows // tile)
    def _(t):
        rows = pl.ds(pl.multiple_of(t * tile, tile), tile)
        q = q_ref[rows, :]

        def step(carry, k, v, mask):
            top, den, num = carry
            s = lax.dot_general(q, k, (((1,), (1,)), ((), ())), preferred_element_type=jnp.float32)
            s = s * scale_factor
            if mask is not None:
                s = jnp.where(mask > 0.5, s, negative_fill)
            new_top = jnp.maximum(top, jnp.max(s, axis=1, keepdims=True))
            factor = jnp.exp(top - new_top)
            w = jnp.exp(s - new_top)
            den = den * factor + jnp.sum(w, axis=1, keepdims=True)
            num = num * factor + jnp.dot(
                w.astype(jnp.bfloat16), v, preferred_element_type=jnp.float32
            )
            return new_top, den, num

        def key_block(b, carry):
            keys = pl.ds(pl.multiple_of(b * block, block), block)
            return step(carry, k_ref[keys, :], v_ref[keys, :], None)

        carry = (
            jnp.full((tile, 1), negative_fill, jnp.float32),
            jnp.zeros((tile, 1), jnp.float32),
            jnp.zeros((tile, HEAD_WIDTH), jnp.float32),
        )
        carry = lax.fori_loop(0, blocks, key_block, carry)
        mask = mask_ref[pl.ds(pl.multiple_of(t * (tile // GROUP), tile // GROUP), tile // GROUP), :]
        mask = jnp.broadcast_to(mask[:, None, :], (tile // GROUP, GROUP, mask.shape[1]))
        top, den, num = step(carry, tk_ref[...], tv_ref[...], mask.reshape(tile, mask.shape[2]))
        num_ref[rows, :] = num
        lane = lax.broadcasted_iota(jnp.int32, (tile, HEAD_WIDTH), 1)
        stat_ref[rows, :] = jnp.where(lane < HEAD_WIDTH // 2, top, den)


def body(
    queries,
    prefix_key_heads,
    prefix_value_heads,
    tree_key_heads,
    tree_value_heads,
    token_embed,
    fc_embed,
    fc_feature,
    draft_gain,
    parents,
    accepted,
):
    tree_count, node_count = parents.shape
    owned = queries.shape[0]
    positions = prefix_key_heads.shape[0]
    every_row = tree_count * node_count
    n = lax.axis_size("ctx")
    me = lax.axis_index("ctx")
    members = n // KEY_HEADS
    part_heads = GROUP // members
    own_cols = part_heads * HEAD_WIDTH

    across = [[j * members + m for j in range(KEY_HEADS)] for m in range(members)]
    beside = [[j * members + m for m in range(members)] for j in range(KEY_HEADS)]
    kv = jnp.concatenate(
        [
            x.reshape(positions, KEY_HEADS, HEAD_WIDTH).transpose(1, 0, 2)[:, None]
            for x in (prefix_key_heads, prefix_value_heads)
        ],
        axis=1,
    )
    kv = lax.all_to_all(kv, "ctx", 0, 0, axis_index_groups=across, tiled=True)

    def heads(x, count):
        return x.reshape(owned, KEY_HEADS, count, HEAD_WIDTH).transpose(1, 0, 2, 3).reshape(
            KEY_HEADS, owned * count, HEAD_WIDTH
        )

    shared = jnp.concatenate(
        [heads(queries, GROUP), heads(tree_key_heads, 1), heads(tree_value_heads, 1)], axis=1
    )
    shared = jnp.repeat(shared, members, axis=0)
    embed = token_embed.reshape(owned, n, part_heads, HEAD_WIDTH).transpose(1, 0, 2, 3)
    embed = embed.reshape(n, owned * part_heads, HEAD_WIDTH)
    small = lax.all_to_all(
        jnp.concatenate([shared, embed], axis=1), "ctx", 0, 0, tiled=True
    )
    cut = [owned * GROUP, owned * (GROUP + 1), owned * (GROUP + 2)]
    q, tk, tv, embed = jnp.split(small, cut, axis=1)
    q = q.reshape(every_row * GROUP, HEAD_WIDTH)
    tk = tk.reshape(every_row, HEAD_WIDTH)
    tv = tv.reshape(every_row, HEAD_WIDTH)
    embed_cols = embed.reshape(every_row, own_cols)

    closure = ancestors(parents)
    own_tree = jnp.arange(every_row, dtype=jnp.int32) // node_count
    allowed = jnp.tile(closure.reshape(every_row, node_count).astype(jnp.float32), (1, tree_count))
    allowed = jnp.where(
        (own_tree[:, None] == own_tree[None, :]) & (me % members == 0), allowed, 0.0
    )
    chosen = accepted[:, None] == jnp.arange(node_count, dtype=jnp.int32)[None, :]
    on_path = jnp.max(
        jnp.where(chosen[:, :, None], closure.astype(jnp.float32), 0.0), axis=1
    ).reshape(every_row)
    row_index = jnp.arange(every_row, dtype=jnp.int32)
    rank = jnp.sum(
        jnp.where(row_index[:, None] < row_index[None, :], on_path[:, None], 0.0), axis=0
    ).astype(jnp.int32)
    slots = round_up(tree_count * PATH_ROWS, 16)
    pick = (
        (rank[None, :] == jnp.arange(slots, dtype=jnp.int32)[:, None]) & (on_path[None, :] > 0.5)
    ).astype(jnp.bfloat16)

    num, stat = pl.pallas_call(
        functools.partial(attention_kernel, positions),
        out_shape=[jax.ShapeDtypeStruct((every_row * GROUP, HEAD_WIDTH), jnp.float32)] * 2,
        compiler_params=pltpu.CompilerParams(vmem_limit_bytes=48 * 1024 * 1024),
    )(
        q,
        kv[:, 0].reshape(-1, HEAD_WIDTH),
        kv[:, 1].reshape(-1, HEAD_WIDTH),
        tk,
        tv,
        allowed,
    )
    both = jnp.concatenate([num, stat], axis=1).reshape(
        every_row, members, part_heads, 2 * HEAD_WIDTH
    )
    both = lax.all_to_all(
        both.transpose(1, 0, 2, 3), "ctx", 0, 0, axis_index_groups=beside, tiled=True
    )
    num = both[..., :HEAD_WIDTH]
    top = both[..., HEAD_WIDTH]
    den = both[..., 2 * HEAD_WIDTH - 1]
    factor = jnp.exp(top - jnp.max(top, axis=0)[None])
    num = jnp.sum(num * factor[..., None], axis=0)
    den = jnp.sum(den * factor, axis=0)
    part = (num / den[..., None]).reshape(every_row, own_cols).astype(jnp.bfloat16)
    attended = lax.all_to_all(part, "ctx", 0, 1, tiled=True)

    def compact(x):
        return jnp.dot(pick, x, preferred_element_type=jnp.float32).astype(jnp.bfloat16)

    joined = jnp.dot(compact(embed_cols), fc_embed, preferred_element_type=jnp.float32)
    joined = joined + jnp.dot(compact(part), fc_feature, preferred_element_type=jnp.float32)
    joined = lax.psum(joined, "ctx")
    mean_square = jnp.mean(joined * joined, axis=1, keepdims=True)
    normed = (joined * lax.rsqrt(mean_square + 1e-06) * draft_gain[None, :]).astype(jnp.bfloat16)
    own_pick = lax.dynamic_slice_in_dim(pick, me * owned, owned, 1)
    draft_input = jnp.einsum(
        "sr,sd->rd", own_pick, normed, preferred_element_type=jnp.float32
    ).astype(jnp.bfloat16)
    return (attended, draft_input)


def solution(mesh):
    placed = (
        P(("groups", "ctx"), None),
        P(("groups", "ctx"), None),
        P(("groups", "ctx"), None),
        P(("groups", "ctx"), None),
        P(("groups", "ctx"), None),
        P(("groups", "ctx"), None),
        P("ctx", None),
        P("ctx", None),
        P(),
        P("groups", None),
        P("groups"),
    )
    return jax.shard_map(
        body,
        mesh=mesh,
        in_specs=placed,
        out_specs=(P(("groups", "ctx"), None), P(("groups", "ctx"), None)),
        check_vma=False,
    )
```

```python
import functools

import jax
import jax.numpy as jnp
from jax import lax
from jax.experimental import pallas as pl
from jax.experimental.pallas import tpu as pltpu
from jax.sharding import PartitionSpec as P

QUERY_HEADS = 64
KEY_HEADS = 8
HEAD_WIDTH = 128
GROUP = QUERY_HEADS // KEY_HEADS
PATH_ROWS = 7
negative_fill = -1e30


def round_up(value, step):
    return (value + step - 1) // step * step


def ancestors(parents):
    nodes = parents.shape[1]
    column = jnp.arange(nodes, dtype=jnp.int32)
    upward = parents[:, :, None] == column[None, None, :]
    closure = (upward | jnp.eye(nodes, dtype=bool)[None]).astype(jnp.bfloat16)
    for repeat in range((PATH_ROWS - 1).bit_length()):
        counts = jnp.einsum("tij,tjk->tik", closure, closure, preferred_element_type=jnp.float32)
        closure = jnp.minimum(counts, 1.0).astype(jnp.bfloat16)
    return closure


def greet(n, me):
    barrier = pltpu.get_barrier_semaphore()

    @pl.loop(1, n)
    def _(r):
        pl.semaphore_signal(
            barrier, inc=1, device_id={"ctx": lax.rem(me + r, n)}, device_id_type=pl.DeviceIdType.MESH
        )

    pl.semaphore_wait(barrier, n - 1)


def push(source, target, send_sem, recv_sem, device):
    return pltpu.make_async_remote_copy(
        src_ref=source,
        dst_ref=target,
        send_sem=send_sem,
        recv_sem=recv_sem,
        device_id={"ctx": device},
        device_id_type=pl.DeviceIdType.MESH,
    )


def attention_kernel(
    n,
    q_rows,
    tree_rows,
    small_ref,
    k_ref,
    v_ref,
    mask_ref,
    num_ref,
    stat_ref,
    embed_ref,
    small,
    keys,
    values,
    tree_k,
    tree_v,
    top_ref,
    den_ref,
    small_send,
    small_recv,
    kv_send,
    kv_recv,
    local_sem,
):
    scale_factor = HEAD_WIDTH ** (-0.5)
    members = n // KEY_HEADS
    me = lax.axis_index("ctx")
    mine = me // members
    member = lax.rem(me, members)
    greet(n, me)

    def small_copy(r):
        to = lax.rem(me + r, n)
        return push(small_ref.at[to], small.at[me], small_send.at[r], small_recv.at[me], to)

    def head_of(ref, j):
        return ref.at[:, pl.ds(pl.multiple_of(j * HEAD_WIDTH, HEAD_WIDTH), HEAD_WIDTH)]

    def kv_copy(r, which):
        j = lax.rem(mine + r, KEY_HEADS)
        source, target = ((k_ref, keys), (v_ref, values))[which]
        return push(
            head_of(source, j),
            target.at[mine],
            kv_send.at[which, r],
            kv_recv.at[which, mine],
            j * members + member,
        )

    @pl.loop(1, n)
    def _(r):
        small_copy(r).start()

    @pl.loop(1, KEY_HEADS)
    def _(r):
        kv_copy(r, 0).start()
        kv_copy(r, 1).start()

    own = [
        pltpu.make_async_copy(small_ref.at[me], small.at[me], local_sem.at[0]),
        pltpu.make_async_copy(head_of(k_ref, mine), keys.at[mine], local_sem.at[1]),
        pltpu.make_async_copy(head_of(v_ref, mine), values.at[mine], local_sem.at[2]),
    ]
    for copy in own:
        copy.start()
    for copy in own:
        copy.wait()

    @pl.loop(1, n)
    def _(r):
        source = lax.rem(me - r + n, n)
        push(
            small_ref.at[source], small.at[source], small_send.at[r], small_recv.at[source], source
        ).wait_recv()

    stack = max(1, 256 // q_rows)
    tile = stack * q_rows
    rows_of_tile = tile // GROUP

    def step(t, k, v, mask, first):
        rows = pl.ds(pl.multiple_of(t * tile, tile), tile)
        q = small[pl.ds(t * stack, stack), 0:q_rows, :].reshape(tile, HEAD_WIDTH)
        s = lax.dot_general(q, k, (((1,), (1,)), ((), ())), preferred_element_type=jnp.float32)
        s = s * scale_factor
        if mask is not None:
            s = jnp.where(mask > 0.5, s, negative_fill)
        highest_here = jnp.max(s, axis=1, keepdims=True)
        if first:
            new_top = highest_here
        else:
            top = top_ref[rows, :]
            new_top = jnp.maximum(top, highest_here)
            factor = jnp.exp(top - new_top)
        w = jnp.exp(s - new_top)
        den = jnp.sum(w, axis=1, keepdims=True)
        num = jnp.dot(w.astype(jnp.bfloat16), v, preferred_element_type=jnp.float32)
        if not first:
            den = den + den_ref[rows, :] * factor
            num = num + num_ref[rows, :] * factor
        top_ref[rows, :] = new_top
        den_ref[rows, :] = den
        num_ref[rows, :] = num

    tree_k[...] = small[:, q_rows : q_rows + tree_rows, :].reshape(tree_k.shape)
    tree_v[...] = small[:, q_rows + tree_rows : q_rows + 2 * tree_rows, :].reshape(tree_v.shape)
    embed_ref[...] = small[:, q_rows + 2 * tree_rows :, :]
    tiles = n // stack

    @pl.loop(0, tiles)
    def _(t):
        start = pl.multiple_of(t * rows_of_tile, rows_of_tile)
        mask = mask_ref[pl.ds(start, rows_of_tile), :]
        mask = jnp.broadcast_to(mask[:, None, :], (rows_of_tile, GROUP, mask.shape[1]))
        step(t, tree_k[...], tree_v[...], mask.reshape(tile, mask.shape[2]), True)

    @pl.loop(0, KEY_HEADS)
    def _(r):
        j = lax.rem(mine - r + KEY_HEADS, KEY_HEADS)

        @pl.when(r > 0)
        def _():
            source = j * members + member
            for which, target in ((0, keys), (1, values)):
                push(
                    target.at[j], target.at[j], kv_send.at[which, r], kv_recv.at[which, j], source
                ).wait_recv()

        @pl.loop(0, tiles)
        def _(t):
            step(t, keys[j], values[j], None, False)

    lane = lax.broadcasted_iota(jnp.int32, stat_ref.shape, 1)
    stat_ref[...] = jnp.where(lane < HEAD_WIDTH // 2, top_ref[...], den_ref[...])

    @pl.loop(1, n)
    def _(r):
        small_copy(r).wait_send()

    @pl.loop(1, KEY_HEADS)
    def _(r):
        kv_copy(r, 0).wait_send()
        kv_copy(r, 1).wait_send()


def join_kernel(
    n, joined_ref, gain_ref, pick_ref, out_ref, pieces, sums, send_a, recv_a, send_b, recv_b
):
    me = lax.axis_index("ctx")
    width = pieces.shape[2]
    greet(n, me)

    def columns(d):
        return joined_ref.at[:, pl.ds(pl.multiple_of(d * width, width), width)]

    def piece(r):
        to = lax.rem(me + r, n)
        return push(columns(to), pieces.at[me], send_a.at[r], recv_a.at[me], to)

    def total(r):
        to = lax.rem(me + r, n)
        return push(sums.at[me], sums.at[me], send_b.at[r], recv_b.at[me], to)

    @pl.loop(1, n)
    def _(r):
        piece(r).start()

    pieces[me] = joined_ref[:, pl.ds(pl.multiple_of(me * width, width), width)]

    @pl.loop(1, n)
    def _(r):
        source = lax.rem(me - r + n, n)
        push(pieces.at[source], pieces.at[source], send_a.at[r], recv_a.at[source], source).wait_recv()

    sums[me] = jnp.sum(pieces[...], axis=0)

    @pl.loop(1, n)
    def _(r):
        total(r).start()

    @pl.loop(1, n)
    def _(r):
        source = lax.rem(me - r + n, n)
        push(sums.at[source], sums.at[source], send_b.at[r], recv_b.at[source], source).wait_recv()

    joined = sums[...]
    squares = jnp.sum(jnp.sum(joined * joined, axis=0), axis=1, keepdims=True)
    inverse = lax.rsqrt(squares / (n * width) + 1e-06)
    for d in range(n):
        normed = sums[d] * inverse * gain_ref[:, d * width : (d + 1) * width]
        out_ref[:, d * width : (d + 1) * width] = jnp.dot(
            pick_ref[...], normed.astype(jnp.bfloat16), preferred_element_type=jnp.float32
        ).astype(jnp.bfloat16)

    @pl.loop(1, n)
    def _(r):
        piece(r).wait_send()
        total(r).wait_send()


def body(
    queries,
    prefix_key_heads,
    prefix_value_heads,
    tree_key_heads,
    tree_value_heads,
    token_embed,
    fc_embed,
    fc_feature,
    draft_gain,
    parents,
    accepted,
):
    tree_count, node_count = parents.shape
    owned = queries.shape[0]
    positions = prefix_key_heads.shape[0]
    every_row = tree_count * node_count
    n = lax.axis_size("ctx")
    me = lax.axis_index("ctx")
    members = n // KEY_HEADS
    part_heads = GROUP // members
    own_cols = part_heads * HEAD_WIDTH

    beside = [[j * members + m for m in range(members)] for j in range(KEY_HEADS)]
    q_rows = owned * GROUP
    tree_rows = round_up(owned, 16)

    def pieces_of(x, parts, count, rows):
        x = x.reshape(owned, parts, count, HEAD_WIDTH).transpose(1, 0, 2, 3)
        x = x.reshape(parts, owned * count, HEAD_WIDTH)
        return jnp.pad(x, ((0, 0), (0, rows - owned * count), (0, 0)))

    shared = jnp.concatenate(
        [
            pieces_of(queries, KEY_HEADS, GROUP, q_rows),
            pieces_of(tree_key_heads, KEY_HEADS, 1, tree_rows),
            pieces_of(tree_value_heads, KEY_HEADS, 1, tree_rows),
        ],
        axis=1,
    )
    embed_rows = round_up(owned * part_heads, 16)
    small = jnp.concatenate(
        [
            jnp.repeat(shared, members, axis=0),
            pieces_of(token_embed, n, part_heads, embed_rows),
        ],
        axis=1,
    )

    closure = ancestors(parents)
    own_tree = jnp.arange(every_row, dtype=jnp.int32) // node_count
    allowed = jnp.tile(closure.reshape(every_row, node_count).astype(jnp.float32), (1, tree_count))
    allowed = jnp.where(
        (own_tree[:, None] == own_tree[None, :]) & (me % members == 0), allowed, 0.0
    )
    chosen = accepted[:, None] == jnp.arange(node_count, dtype=jnp.int32)[None, :]
    on_path = jnp.max(
        jnp.where(chosen[:, :, None], closure.astype(jnp.float32), 0.0), axis=1
    ).reshape(every_row)
    row_index = jnp.arange(every_row, dtype=jnp.int32)
    rank = jnp.sum(
        jnp.where(row_index[:, None] < row_index[None, :], on_path[:, None], 0.0), axis=0
    ).astype(jnp.int32)
    slots = round_up(tree_count * PATH_ROWS, 16)
    pick = (
        (rank[None, :] == jnp.arange(slots, dtype=jnp.int32)[:, None]) & (on_path[None, :] > 0.5)
    ).astype(jnp.bfloat16)

    allowed = jnp.pad(
        allowed.reshape(every_row, n, owned), ((0, 0), (0, 0), (0, tree_rows - owned))
    ).reshape(every_row, n * tree_rows)
    any_space = pl.BlockSpec(memory_space=pl.ANY)
    in_vmem = pl.BlockSpec(memory_space=pltpu.VMEM)
    num, stat, embed = pl.pallas_call(
        functools.partial(attention_kernel, n, q_rows, tree_rows),
        out_shape=[
            jax.ShapeDtypeStruct((every_row * GROUP, HEAD_WIDTH), jnp.float32),
            jax.ShapeDtypeStruct((every_row * GROUP, HEAD_WIDTH), jnp.float32),
            jax.ShapeDtypeStruct((n, embed_rows, HEAD_WIDTH), jnp.bfloat16),
        ],
        in_specs=[any_space] * 3 + [in_vmem],
        out_specs=[in_vmem] * 3,
        scratch_shapes=[
            pltpu.VMEM(small.shape, jnp.bfloat16),
            pltpu.VMEM((KEY_HEADS, positions, HEAD_WIDTH), jnp.bfloat16),
            pltpu.VMEM((KEY_HEADS, positions, HEAD_WIDTH), jnp.bfloat16),
            pltpu.VMEM((n * tree_rows, HEAD_WIDTH), jnp.bfloat16),
            pltpu.VMEM((n * tree_rows, HEAD_WIDTH), jnp.bfloat16),
            pltpu.VMEM((every_row * GROUP, 1), jnp.float32),
            pltpu.VMEM((every_row * GROUP, 1), jnp.float32),
            pltpu.SemaphoreType.DMA((n,)),
            pltpu.SemaphoreType.DMA((n,)),
            pltpu.SemaphoreType.DMA((2, KEY_HEADS)),
            pltpu.SemaphoreType.DMA((2, KEY_HEADS)),
            pltpu.SemaphoreType.DMA((3,)),
        ],
        compiler_params=pltpu.CompilerParams(
            collective_id=0, has_side_effects=True, vmem_limit_bytes=40 * 1024 * 1024
        ),
        cost_estimate=pl.CostEstimate(
            flops=4 * every_row * GROUP * positions * KEY_HEADS * HEAD_WIDTH,
            bytes_accessed=4 * prefix_key_heads.size,
            transcendentals=every_row * GROUP * positions * KEY_HEADS,
        ),
    )(small, prefix_key_heads, prefix_value_heads, allowed)
    embed_cols = embed[:, : owned * part_heads].reshape(every_row, own_cols)
    both = jnp.concatenate([num, stat], axis=1).reshape(
        every_row, members, part_heads, 2 * HEAD_WIDTH
    )
    both = lax.all_to_all(
        both.transpose(1, 0, 2, 3), "ctx", 0, 0, axis_index_groups=beside, tiled=True
    )
    num = both[..., :HEAD_WIDTH]
    top = both[..., HEAD_WIDTH]
    den = both[..., 2 * HEAD_WIDTH - 1]
    factor = jnp.exp(top - jnp.max(top, axis=0)[None])
    num = jnp.sum(num * factor[..., None], axis=0)
    den = jnp.sum(den * factor, axis=0)
    part = (num / den[..., None]).reshape(every_row, own_cols).astype(jnp.bfloat16)
    attended = lax.all_to_all(part, "ctx", 0, 1, tiled=True)

    def compact(x):
        return jnp.dot(pick, x, preferred_element_type=jnp.float32).astype(jnp.bfloat16)

    joined = jnp.dot(compact(embed_cols), fc_embed, preferred_element_type=jnp.float32)
    joined = joined + jnp.dot(compact(part), fc_feature, preferred_element_type=jnp.float32)
    own_pick = lax.dynamic_slice_in_dim(pick, me * owned, owned, 1).T
    width = joined.shape[1] // n
    draft_input = pl.pallas_call(
        functools.partial(join_kernel, n),
        out_shape=jax.ShapeDtypeStruct(token_embed.shape, jnp.bfloat16),
        in_specs=[in_vmem] * 3,
        out_specs=in_vmem,
        scratch_shapes=[
            pltpu.VMEM((n, slots, width), jnp.float32),
            pltpu.VMEM((n, slots, width), jnp.float32),
            pltpu.SemaphoreType.DMA((n,)),
            pltpu.SemaphoreType.DMA((n,)),
            pltpu.SemaphoreType.DMA((n,)),
            pltpu.SemaphoreType.DMA((n,)),
        ],
        compiler_params=pltpu.CompilerParams(
            collective_id=1, has_side_effects=True, vmem_limit_bytes=24 * 1024 * 1024
        ),
    )(joined, draft_gain[None, :], own_pick)
    return (attended, draft_input)


def solution(mesh):
    placed = (
        P(("groups", "ctx"), None),
        P(("groups", "ctx"), None),
        P(("groups", "ctx"), None),
        P(("groups", "ctx"), None),
        P(("groups", "ctx"), None),
        P(("groups", "ctx"), None),
        P("ctx", None),
        P("ctx", None),
        P(),
        P("groups", None),
        P("groups"),
    )
    return jax.shard_map(
        body,
        mesh=mesh,
        in_specs=placed,
        out_specs=(P(("groups", "ctx"), None), P(("groups", "ctx"), None)),
        check_vma=False,
    )
```

```python
import functools

import jax
import jax.numpy as jnp
from jax import lax
from jax.experimental import pallas as pl
from jax.experimental.pallas import tpu as pltpu
from jax.sharding import PartitionSpec as P

QUERY_HEADS = 64
KEY_HEADS = 8
HEAD_WIDTH = 128
GROUP = QUERY_HEADS // KEY_HEADS
PATH_ROWS = 7
negative_fill = -1e30


def round_up(value, step):
    return (value + step - 1) // step * step


def ancestors(parents):
    nodes = parents.shape[1]
    column = jnp.arange(nodes, dtype=jnp.int32)
    upward = parents[:, :, None] == column[None, None, :]
    closure = (upward | jnp.eye(nodes, dtype=bool)[None]).astype(jnp.bfloat16)
    for repeat in range((PATH_ROWS - 1).bit_length()):
        counts = jnp.einsum("tij,tjk->tik", closure, closure, preferred_element_type=jnp.float32)
        closure = jnp.minimum(counts, 1.0).astype(jnp.bfloat16)
    return closure


def greet(n, me):
    barrier = pltpu.get_barrier_semaphore()

    @pl.loop(1, n)
    def _(r):
        pl.semaphore_signal(
            barrier, inc=1, device_id={"ctx": lax.rem(me + r, n)}, device_id_type=pl.DeviceIdType.MESH
        )

    pl.semaphore_wait(barrier, n - 1)


def push(source, target, send_sem, recv_sem, device):
    return pltpu.make_async_remote_copy(
        src_ref=source,
        dst_ref=target,
        send_sem=send_sem,
        recv_sem=recv_sem,
        device_id={"ctx": device},
        device_id_type=pl.DeviceIdType.MESH,
    )


def attention_kernel(
    n,
    q_rows,
    tree_rows,
    small_ref,
    k_ref,
    v_ref,
    mask_ref,
    num_ref,
    stat_ref,
    embed_ref,
    small,
    keys,
    values,
    tree_k,
    tree_v,
    top_ref,
    den_ref,
    small_send,
    small_recv,
    kv_send,
    kv_recv,
    local_sem,
):
    scale_factor = HEAD_WIDTH ** (-0.5)
    members = n // KEY_HEADS
    me = lax.axis_index("ctx")
    mine = me // members
    member = lax.rem(me, members)
    greet(n, me)

    def small_copy(r):
        to = lax.rem(me + r, n)
        return push(small_ref.at[to], small.at[me], small_send.at[r], small_recv.at[me], to)

    def head_of(ref, j):
        return ref.at[:, pl.ds(pl.multiple_of(j * HEAD_WIDTH, HEAD_WIDTH), HEAD_WIDTH)]

    def kv_copy(r, which):
        j = lax.rem(mine + r, KEY_HEADS)
        source, target = ((k_ref, keys), (v_ref, values))[which]
        return push(
            head_of(source, j),
            target.at[mine],
            kv_send.at[which, r],
            kv_recv.at[which, mine],
            j * members + member,
        )

    @pl.loop(1, n)
    def _(r):
        small_copy(r).start()

    @pl.loop(1, KEY_HEADS)
    def _(r):
        kv_copy(r, 0).start()
        kv_copy(r, 1).start()

    own = [
        pltpu.make_async_copy(small_ref.at[me], small.at[me], local_sem.at[0]),
        pltpu.make_async_copy(head_of(k_ref, mine), keys.at[mine], local_sem.at[1]),
        pltpu.make_async_copy(head_of(v_ref, mine), values.at[mine], local_sem.at[2]),
    ]
    for copy in own:
        copy.start()
    for copy in own:
        copy.wait()

    @pl.loop(1, n)
    def _(r):
        source = lax.rem(me - r + n, n)
        push(
            small_ref.at[source], small.at[source], small_send.at[r], small_recv.at[source], source
        ).wait_recv()

    stack = max(1, 256 // q_rows)
    tile = stack * q_rows
    rows_of_tile = tile // GROUP

    def step(t, k, v, mask, first):
        rows = pl.ds(pl.multiple_of(t * tile, tile), tile)
        q = small[pl.ds(t * stack, stack), 0:q_rows, :].reshape(tile, HEAD_WIDTH)
        s = lax.dot_general(q, k, (((1,), (1,)), ((), ())), preferred_element_type=jnp.float32)
        s = s * scale_factor
        if mask is not None:
            s = jnp.where(mask > 0.5, s, negative_fill)
        highest_here = jnp.max(s, axis=1, keepdims=True)
        if first:
            new_top = highest_here
        else:
            top = top_ref[rows, :]
            new_top = jnp.maximum(top, highest_here)
            factor = jnp.exp(top - new_top)
        w = jnp.exp(s - new_top)
        den = jnp.sum(w, axis=1, keepdims=True)
        num = jnp.dot(w.astype(jnp.bfloat16), v, preferred_element_type=jnp.float32)
        if not first:
            den = den + den_ref[rows, :] * factor
            num = num + num_ref[rows, :] * factor
        top_ref[rows, :] = new_top
        den_ref[rows, :] = den
        num_ref[rows, :] = num

    tree_k[...] = small[:, q_rows : q_rows + tree_rows, :].reshape(tree_k.shape)
    tree_v[...] = small[:, q_rows + tree_rows : q_rows + 2 * tree_rows, :].reshape(tree_v.shape)
    embed_ref[...] = small[:, q_rows + 2 * tree_rows :, :]
    tiles = n // stack

    @pl.loop(0, tiles)
    def _(t):
        start = pl.multiple_of(t * rows_of_tile, rows_of_tile)
        mask = mask_ref[pl.ds(start, rows_of_tile), :]
        mask = jnp.broadcast_to(mask[:, None, :], (rows_of_tile, GROUP, mask.shape[1]))
        step(t, tree_k[...], tree_v[...], mask.reshape(tile, mask.shape[2]), True)

    @pl.loop(0, KEY_HEADS)
    def _(r):
        j = lax.rem(mine - r + KEY_HEADS, KEY_HEADS)

        @pl.when(r > 0)
        def _():
            source = j * members + member
            for which, target in ((0, keys), (1, values)):
                push(
                    target.at[j], target.at[j], kv_send.at[which, r], kv_recv.at[which, j], source
                ).wait_recv()

        @pl.loop(0, tiles)
        def _(t):
            step(t, keys[j], values[j], None, False)

    lane = lax.broadcasted_iota(jnp.int32, stat_ref.shape, 1)
    stat_ref[...] = jnp.where(lane < HEAD_WIDTH // 2, top_ref[...], den_ref[...])

    @pl.loop(1, n)
    def _(r):
        small_copy(r).wait_send()

    @pl.loop(1, KEY_HEADS)
    def _(r):
        kv_copy(r, 0).wait_send()
        kv_copy(r, 1).wait_send()


def join_kernel(
    n,
    pick_ref,
    joined_ref,
    gain_ref,
    part_ref,
    draft_ref,
    attended_ref,
    pieces,
    rows,
    attended,
    send_a,
    recv_a,
    send_b,
    recv_b,
    send_c,
    recv_c,
):
    me = lax.axis_index("ctx")
    slots = joined_ref.shape[0]
    greet(n, me)

    def piece(r):
        to = lax.rem(me + r, n)
        return push(joined_ref.at[to], pieces.at[me], send_a.at[r], recv_a.at[me], to)

    def finished(r):
        to = lax.rem(me + r, n)
        return push(rows.at[me], rows.at[me], send_b.at[r], recv_b.at[me], to)

    def part(r):
        to = lax.rem(me + r, n)
        return push(part_ref.at[to], attended.at[me], send_c.at[r], recv_c.at[me], to)

    @pl.loop(1, n)
    def _(r):
        @pl.when(lax.rem(me + r, n) < slots)
        def _():
            piece(r).start()

    @pl.loop(1, n)
    def _(r):
        part(r).start()

    attended[me] = part_ref[me]

    @pl.when(me < slots)
    def _():
        pieces[me] = joined_ref[me]

        @pl.loop(1, n)
        def _(r):
            source = lax.rem(me - r + n, n)
            push(
                pieces.at[source], pieces.at[source], send_a.at[r], recv_a.at[source], source
            ).wait_recv()

        joined = jnp.sum(pieces[...], axis=0)
        squares = jnp.sum(jnp.sum(joined * joined, axis=0, keepdims=True), axis=1, keepdims=True)
        inverse = lax.rsqrt(squares / joined.size + 1e-06)
        rows[me] = (joined * inverse * gain_ref[...]).astype(jnp.bfloat16)

        @pl.loop(1, n)
        def _(r):
            finished(r).start()

    @pl.loop(1, n)
    def _(r):
        source = lax.rem(me - r + n, n)
        push(
            attended.at[source], attended.at[source], send_c.at[r], recv_c.at[source], source
        ).wait_recv()

    attended_ref[...] = attended[...]

    @pl.loop(1, n)
    def _(r):
        source = lax.rem(me - r + n, n)

        @pl.when(source < slots)
        def _():
            push(
                rows.at[source], rows.at[source], send_b.at[r], recv_b.at[source], source
            ).wait_recv()

    for row in range(draft_ref.shape[0]):
        total = jnp.zeros(draft_ref.shape[1:], jnp.float32)
        for slot in range(slots):
            total = total + pick_ref[row, slot] * rows[slot].astype(jnp.float32)
        draft_ref[row] = total.astype(jnp.bfloat16)

    @pl.loop(1, n)
    def _(r):
        @pl.when(lax.rem(me + r, n) < slots)
        def _():
            piece(r).wait_send()

        part(r).wait_send()

        @pl.when(me < slots)
        def _():
            finished(r).wait_send()


def body(
    queries,
    prefix_key_heads,
    prefix_value_heads,
    tree_key_heads,
    tree_value_heads,
    token_embed,
    fc_embed,
    fc_feature,
    draft_gain,
    parents,
    accepted,
):
    tree_count, node_count = parents.shape
    owned = queries.shape[0]
    positions = prefix_key_heads.shape[0]
    every_row = tree_count * node_count
    n = lax.axis_size("ctx")
    me = lax.axis_index("ctx")
    members = n // KEY_HEADS
    part_heads = GROUP // members
    own_cols = part_heads * HEAD_WIDTH

    beside = [[j * members + m for m in range(members)] for j in range(KEY_HEADS)]
    q_rows = owned * GROUP
    tree_rows = round_up(owned, 16)

    def pieces_of(x, parts, count, rows):
        x = x.reshape(owned, parts, count, HEAD_WIDTH).transpose(1, 0, 2, 3)
        x = x.reshape(parts, owned * count, HEAD_WIDTH)
        return jnp.pad(x, ((0, 0), (0, rows - owned * count), (0, 0)))

    shared = jnp.concatenate(
        [
            pieces_of(queries, KEY_HEADS, GROUP, q_rows),
            pieces_of(tree_key_heads, KEY_HEADS, 1, tree_rows),
            pieces_of(tree_value_heads, KEY_HEADS, 1, tree_rows),
        ],
        axis=1,
    )
    embed_rows = round_up(owned * part_heads, 16)
    small = jnp.concatenate(
        [
            jnp.repeat(shared, members, axis=0),
            pieces_of(token_embed, n, part_heads, embed_rows),
        ],
        axis=1,
    )

    closure = ancestors(parents)
    own_tree = jnp.arange(every_row, dtype=jnp.int32) // node_count
    allowed = jnp.tile(closure.reshape(every_row, node_count).astype(jnp.float32), (1, tree_count))
    allowed = jnp.where(
        (own_tree[:, None] == own_tree[None, :]) & (me % members == 0), allowed, 0.0
    )
    chosen = accepted[:, None] == jnp.arange(node_count, dtype=jnp.int32)[None, :]
    on_path = jnp.max(
        jnp.where(chosen[:, :, None], closure.astype(jnp.float32), 0.0), axis=1
    ).reshape(every_row)
    row_index = jnp.arange(every_row, dtype=jnp.int32)
    rank = jnp.sum(
        jnp.where(row_index[:, None] < row_index[None, :], on_path[:, None], 0.0), axis=0
    ).astype(jnp.int32)
    slots = round_up(tree_count * PATH_ROWS, 16)
    pick = (
        (rank[None, :] == jnp.arange(slots, dtype=jnp.int32)[:, None]) & (on_path[None, :] > 0.5)
    ).astype(jnp.bfloat16)

    allowed = jnp.pad(
        allowed.reshape(every_row, n, owned), ((0, 0), (0, 0), (0, tree_rows - owned))
    ).reshape(every_row, n * tree_rows)
    any_space = pl.BlockSpec(memory_space=pl.ANY)
    in_vmem = pl.BlockSpec(memory_space=pltpu.VMEM)
    num, stat, embed = pl.pallas_call(
        functools.partial(attention_kernel, n, q_rows, tree_rows),
        out_shape=[
            jax.ShapeDtypeStruct((every_row * GROUP, HEAD_WIDTH), jnp.float32),
            jax.ShapeDtypeStruct((every_row * GROUP, HEAD_WIDTH), jnp.float32),
            jax.ShapeDtypeStruct((n, embed_rows, HEAD_WIDTH), jnp.bfloat16),
        ],
        in_specs=[any_space] * 3 + [in_vmem],
        out_specs=[in_vmem] * 3,
        scratch_shapes=[
            pltpu.VMEM(small.shape, jnp.bfloat16),
            pltpu.VMEM((KEY_HEADS, positions, HEAD_WIDTH), jnp.bfloat16),
            pltpu.VMEM((KEY_HEADS, positions, HEAD_WIDTH), jnp.bfloat16),
            pltpu.VMEM((n * tree_rows, HEAD_WIDTH), jnp.bfloat16),
            pltpu.VMEM((n * tree_rows, HEAD_WIDTH), jnp.bfloat16),
            pltpu.VMEM((every_row * GROUP, 1), jnp.float32),
            pltpu.VMEM((every_row * GROUP, 1), jnp.float32),
            pltpu.SemaphoreType.DMA((n,)),
            pltpu.SemaphoreType.DMA((n,)),
            pltpu.SemaphoreType.DMA((2, KEY_HEADS)),
            pltpu.SemaphoreType.DMA((2, KEY_HEADS)),
            pltpu.SemaphoreType.DMA((3,)),
        ],
        compiler_params=pltpu.CompilerParams(
            collective_id=0, has_side_effects=True, vmem_limit_bytes=40 * 1024 * 1024
        ),
        cost_estimate=pl.CostEstimate(
            flops=4 * every_row * GROUP * positions * KEY_HEADS * HEAD_WIDTH,
            bytes_accessed=4 * prefix_key_heads.size,
            transcendentals=every_row * GROUP * positions * KEY_HEADS,
        ),
    )(small, prefix_key_heads, prefix_value_heads, allowed)
    embed_cols = embed[:, : owned * part_heads].reshape(every_row, own_cols)
    both = jnp.concatenate([num, stat], axis=1).reshape(
        every_row, members, part_heads, 2 * HEAD_WIDTH
    )
    both = lax.all_to_all(
        both.transpose(1, 0, 2, 3), "ctx", 0, 0, axis_index_groups=beside, tiled=True
    )
    num = both[..., :HEAD_WIDTH]
    top = both[..., HEAD_WIDTH]
    den = both[..., 2 * HEAD_WIDTH - 1]
    factor = jnp.exp(top - jnp.max(top, axis=0)[None])
    num = jnp.sum(num * factor[..., None], axis=0)
    den = jnp.sum(den * factor, axis=0)
    part = (num / den[..., None]).reshape(every_row, own_cols).astype(jnp.bfloat16)
    parts = jnp.pad(
        part.reshape(n, owned * part_heads, HEAD_WIDTH),
        ((0, 0), (0, embed_rows - owned * part_heads), (0, 0)),
    )

    def compact(x):
        return jnp.dot(pick, x, preferred_element_type=jnp.float32).astype(jnp.bfloat16)

    joined = jnp.dot(compact(embed_cols), fc_embed, preferred_element_type=jnp.float32)
    joined = joined + jnp.dot(compact(part), fc_feature, preferred_element_type=jnp.float32)
    own_pick = lax.dynamic_slice_in_dim(pick, me * owned, owned, 1).T.astype(jnp.float32)
    lanes = (joined.shape[1] // HEAD_WIDTH, HEAD_WIDTH)
    draft, arrived = pl.pallas_call(
        functools.partial(join_kernel, n),
        out_shape=[
            jax.ShapeDtypeStruct((owned,) + lanes, jnp.bfloat16),
            jax.ShapeDtypeStruct(parts.shape, jnp.bfloat16),
        ],
        in_specs=[pl.BlockSpec(memory_space=pltpu.SMEM)] + [in_vmem] * 3,
        out_specs=[in_vmem] * 2,
        scratch_shapes=[
            pltpu.VMEM((n,) + lanes, jnp.float32),
            pltpu.VMEM((slots,) + lanes, jnp.bfloat16),
            pltpu.VMEM(parts.shape, jnp.bfloat16),
        ]
        + [pltpu.SemaphoreType.DMA((n,))] * 6,
        compiler_params=pltpu.CompilerParams(
            collective_id=1, has_side_effects=True, vmem_limit_bytes=24 * 1024 * 1024
        ),
    )(own_pick, joined.reshape((slots,) + lanes), draft_gain.reshape(lanes), parts)
    draft_input = draft.reshape(owned, -1)
    attended = arrived[:, : owned * part_heads].reshape(n, owned, own_cols)
    attended = attended.transpose(1, 0, 2).reshape(owned, -1)
    return (attended, draft_input)


def solution(mesh):
    placed = (
        P(("groups", "ctx"), None),
        P(("groups", "ctx"), None),
        P(("groups", "ctx"), None),
        P(("groups", "ctx"), None),
        P(("groups", "ctx"), None),
        P(("groups", "ctx"), None),
        P("ctx", None),
        P("ctx", None),
        P(),
        P("groups", None),
        P("groups"),
    )
    return jax.shard_map(
        body,
        mesh=mesh,
        in_specs=placed,
        out_specs=(P(("groups", "ctx"), None), P(("groups", "ctx"), None)),
        check_vma=False,
    )
```

```python
import functools

import jax
import jax.numpy as jnp
from jax import lax
from jax.experimental import pallas as pl
from jax.experimental.pallas import tpu as pltpu
from jax.sharding import PartitionSpec as P

QUERY_HEADS = 64
KEY_HEADS = 8
HEAD_WIDTH = 128
GROUP = QUERY_HEADS // KEY_HEADS
PATH_ROWS = 7
negative_fill = -1e30


def round_up(value, step):
    return (value + step - 1) // step * step


def ancestors(parents):
    nodes = parents.shape[1]
    column = jnp.arange(nodes, dtype=jnp.int32)
    upward = parents[:, :, None] == column[None, None, :]
    closure = (upward | jnp.eye(nodes, dtype=bool)[None]).astype(jnp.bfloat16)
    for repeat in range((PATH_ROWS - 1).bit_length()):
        counts = jnp.einsum("tij,tjk->tik", closure, closure, preferred_element_type=jnp.float32)
        closure = jnp.minimum(counts, 1.0).astype(jnp.bfloat16)
    return closure


def greet(n, me):
    barrier = pltpu.get_barrier_semaphore()

    @pl.loop(1, n)
    def _(r):
        pl.semaphore_signal(
            barrier, inc=1, device_id={"ctx": lax.rem(me + r, n)}, device_id_type=pl.DeviceIdType.MESH
        )

    pl.semaphore_wait(barrier, n - 1)


def push(source, target, send_sem, recv_sem, device):
    return pltpu.make_async_remote_copy(
        src_ref=source,
        dst_ref=target,
        send_sem=send_sem,
        recv_sem=recv_sem,
        device_id={"ctx": device},
        device_id_type=pl.DeviceIdType.MESH,
    )


def attention_kernel(
    n,
    q_rows,
    tree_rows,
    small_ref,
    k_ref,
    v_ref,
    mask_ref,
    expand_ref,
    fc_ref,
    num_ref,
    stat_ref,
    joined_ref,
    small,
    fc,
    keys,
    values,
    tree_k,
    tree_v,
    top_ref,
    den_ref,
    small_send,
    small_recv,
    kv_send,
    kv_recv,
    local_sem,
):
    scale_factor = HEAD_WIDTH ** (-0.5)
    members = n // KEY_HEADS
    me = lax.axis_index("ctx")
    mine = me // members
    member = lax.rem(me, members)
    weights = pltpu.make_async_copy(fc_ref, fc, local_sem.at[3])
    greet(n, me)

    def small_copy(r):
        to = lax.rem(me + r, n)
        return push(small_ref.at[to], small.at[me], small_send.at[r], small_recv.at[me], to)

    def head_of(ref, j):
        return ref.at[:, pl.ds(pl.multiple_of(j * HEAD_WIDTH, HEAD_WIDTH), HEAD_WIDTH)]

    def kv_copy(r, which):
        j = lax.rem(mine + r, KEY_HEADS)
        source, target = ((k_ref, keys), (v_ref, values))[which]
        return push(
            head_of(source, j),
            target.at[mine],
            kv_send.at[which, r],
            kv_recv.at[which, mine],
            j * members + member,
        )

    @pl.loop(1, n)
    def _(r):
        small_copy(r).start()

    @pl.loop(1, KEY_HEADS)
    def _(r):
        kv_copy(r, 0).start()
        kv_copy(r, 1).start()

    own = [
        pltpu.make_async_copy(small_ref.at[me], small.at[me], local_sem.at[0]),
        pltpu.make_async_copy(head_of(k_ref, mine), keys.at[mine], local_sem.at[1]),
        pltpu.make_async_copy(head_of(v_ref, mine), values.at[mine], local_sem.at[2]),
    ]
    for copy in own:
        copy.start()
    weights.start()
    for copy in own:
        copy.wait()

    @pl.loop(1, n)
    def _(r):
        source = lax.rem(me - r + n, n)
        push(
            small_ref.at[source], small.at[source], small_send.at[r], small_recv.at[source], source
        ).wait_recv()

    stack = max(1, 256 // q_rows)
    tile = stack * q_rows
    rows_of_tile = tile // GROUP

    def step(t, k, v, mask, first):
        rows = pl.ds(pl.multiple_of(t * tile, tile), tile)
        q = small[pl.ds(t * stack, stack), 0:q_rows, :].reshape(tile, HEAD_WIDTH)
        s = lax.dot_general(q, k, (((1,), (1,)), ((), ())), preferred_element_type=jnp.float32)
        s = s * scale_factor
        if mask is not None:
            s = jnp.where(mask > 0.5, s, negative_fill)
        highest_here = jnp.max(s, axis=1, keepdims=True)
        if first:
            new_top = highest_here
        else:
            top = top_ref[rows, :]
            new_top = jnp.maximum(top, highest_here)
            factor = jnp.exp(top - new_top)
        w = jnp.exp(s - new_top)
        den = jnp.sum(w, axis=1, keepdims=True)
        num = jnp.dot(w.astype(jnp.bfloat16), v, preferred_element_type=jnp.float32)
        if not first:
            den = den + den_ref[rows, :] * factor
            num = num + num_ref[rows, :] * factor
        top_ref[rows, :] = new_top
        den_ref[rows, :] = den
        num_ref[rows, :] = num

    tree_k[...] = small[:, q_rows : q_rows + tree_rows, :].reshape(tree_k.shape)
    tree_v[...] = small[:, q_rows + tree_rows : q_rows + 2 * tree_rows, :].reshape(tree_v.shape)
    tiles = n // stack

    @pl.loop(0, tiles)
    def _(t):
        start = pl.multiple_of(t * rows_of_tile, rows_of_tile)
        mask = mask_ref[pl.ds(start, rows_of_tile), :]
        mask = jnp.broadcast_to(mask[:, None, :], (rows_of_tile, GROUP, mask.shape[1]))
        step(t, tree_k[...], tree_v[...], mask.reshape(tile, mask.shape[2]), True)

    embed = small[:, q_rows + 2 * tree_rows :, :].reshape(expand_ref.shape[2], HEAD_WIDTH)
    kept = [
        jnp.dot(expand_ref[h], embed, preferred_element_type=jnp.float32).astype(jnp.bfloat16)
        for h in range(expand_ref.shape[0])
    ]
    kept = jnp.concatenate(kept, axis=1)
    weights.wait()
    chunk = 8 * HEAD_WIDTH

    @pl.loop(0, fc.shape[1] // chunk)
    def _(c):
        cols = pl.ds(pl.multiple_of(c * chunk, chunk), chunk)
        joined_ref[:, cols] = jnp.dot(kept, fc[:, cols], preferred_element_type=jnp.float32)

    @pl.loop(0, KEY_HEADS)
    def _(r):
        j = lax.rem(mine - r + KEY_HEADS, KEY_HEADS)

        @pl.when(r > 0)
        def _():
            source = j * members + member
            for which, target in ((0, keys), (1, values)):
                push(
                    target.at[j], target.at[j], kv_send.at[which, r], kv_recv.at[which, j], source
                ).wait_recv()

        @pl.loop(0, tiles)
        def _(t):
            step(t, keys[j], values[j], None, False)

    lane = lax.broadcasted_iota(jnp.int32, stat_ref.shape, 1)
    stat_ref[...] = jnp.where(lane < HEAD_WIDTH // 2, top_ref[...], den_ref[...])

    @pl.loop(1, n)
    def _(r):
        small_copy(r).wait_send()

    @pl.loop(1, KEY_HEADS)
    def _(r):
        kv_copy(r, 0).wait_send()
        kv_copy(r, 1).wait_send()


def join_kernel(
    n,
    pick_ref,
    joined_ref,
    gain_ref,
    part_ref,
    draft_ref,
    attended_ref,
    pieces,
    rows,
    attended,
    send_a,
    recv_a,
    send_b,
    recv_b,
    send_c,
    recv_c,
):
    me = lax.axis_index("ctx")
    slots = joined_ref.shape[0]
    greet(n, me)

    def piece(r):
        to = lax.rem(me + r, n)
        return push(joined_ref.at[to], pieces.at[me], send_a.at[r], recv_a.at[me], to)

    def finished(r):
        to = lax.rem(me + r, n)
        return push(rows.at[me], rows.at[me], send_b.at[r], recv_b.at[me], to)

    def part(r):
        to = lax.rem(me + r, n)
        return push(part_ref.at[to], attended.at[me], send_c.at[r], recv_c.at[me], to)

    @pl.loop(1, n)
    def _(r):
        @pl.when(lax.rem(me + r, n) < slots)
        def _():
            piece(r).start()

    @pl.loop(1, n)
    def _(r):
        part(r).start()

    attended[me] = part_ref[me]

    @pl.when(me < slots)
    def _():
        pieces[me] = joined_ref[me]

        @pl.loop(1, n)
        def _(r):
            source = lax.rem(me - r + n, n)
            push(
                pieces.at[source], pieces.at[source], send_a.at[r], recv_a.at[source], source
            ).wait_recv()

        joined = jnp.sum(pieces[...], axis=0)
        squares = jnp.sum(jnp.sum(joined * joined, axis=0, keepdims=True), axis=1, keepdims=True)
        inverse = lax.rsqrt(squares / joined.size + 1e-06)
        rows[me] = (joined * inverse * gain_ref[...]).astype(jnp.bfloat16)

        @pl.loop(1, n)
        def _(r):
            finished(r).start()

    @pl.loop(1, n)
    def _(r):
        source = lax.rem(me - r + n, n)
        push(
            attended.at[source], attended.at[source], send_c.at[r], recv_c.at[source], source
        ).wait_recv()

    attended_ref[...] = attended[...]

    @pl.loop(1, n)
    def _(r):
        source = lax.rem(me - r + n, n)

        @pl.when(source < slots)
        def _():
            push(
                rows.at[source], rows.at[source], send_b.at[r], recv_b.at[source], source
            ).wait_recv()

    for row in range(draft_ref.shape[0]):
        total = jnp.zeros(draft_ref.shape[1:], jnp.float32)
        for slot in range(slots):
            total = total + pick_ref[row, slot] * rows[slot].astype(jnp.float32)
        draft_ref[row] = total.astype(jnp.bfloat16)

    @pl.loop(1, n)
    def _(r):
        @pl.when(lax.rem(me + r, n) < slots)
        def _():
            piece(r).wait_send()

        part(r).wait_send()

        @pl.when(me < slots)
        def _():
            finished(r).wait_send()


def body(
    queries,
    prefix_key_heads,
    prefix_value_heads,
    tree_key_heads,
    tree_value_heads,
    token_embed,
    fc_embed,
    fc_feature,
    draft_gain,
    parents,
    accepted,
):
    tree_count, node_count = parents.shape
    owned = queries.shape[0]
    positions = prefix_key_heads.shape[0]
    every_row = tree_count * node_count
    n = lax.axis_size("ctx")
    me = lax.axis_index("ctx")
    members = n // KEY_HEADS
    part_heads = GROUP // members
    own_cols = part_heads * HEAD_WIDTH

    beside = [[j * members + m for m in range(members)] for j in range(KEY_HEADS)]
    q_rows = owned * GROUP
    tree_rows = round_up(owned, 16)

    def pieces_of(x, parts, count, rows):
        x = x.reshape(owned, parts, count, HEAD_WIDTH).transpose(1, 0, 2, 3)
        x = x.reshape(parts, owned * count, HEAD_WIDTH)
        return jnp.pad(x, ((0, 0), (0, rows - owned * count), (0, 0)))

    shared = jnp.concatenate(
        [
            pieces_of(queries, KEY_HEADS, GROUP, q_rows),
            pieces_of(tree_key_heads, KEY_HEADS, 1, tree_rows),
            pieces_of(tree_value_heads, KEY_HEADS, 1, tree_rows),
        ],
        axis=1,
    )
    embed_rows = round_up(owned * part_heads, 16)
    small = jnp.concatenate(
        [
            jnp.repeat(shared, members, axis=0),
            pieces_of(token_embed, n, part_heads, embed_rows),
        ],
        axis=1,
    )

    closure = ancestors(parents)
    own_tree = jnp.arange(every_row, dtype=jnp.int32) // node_count
    allowed = jnp.tile(closure.reshape(every_row, node_count).astype(jnp.float32), (1, tree_count))
    allowed = jnp.where(
        (own_tree[:, None] == own_tree[None, :]) & (me % members == 0), allowed, 0.0
    )
    chosen = accepted[:, None] == jnp.arange(node_count, dtype=jnp.int32)[None, :]
    on_path = jnp.max(
        jnp.where(chosen[:, :, None], closure.astype(jnp.float32), 0.0), axis=1
    ).reshape(every_row)
    row_index = jnp.arange(every_row, dtype=jnp.int32)
    rank = jnp.sum(
        jnp.where(row_index[:, None] < row_index[None, :], on_path[:, None], 0.0), axis=0
    ).astype(jnp.int32)
    slots = round_up(tree_count * PATH_ROWS, 16)
    pick = (
        (rank[None, :] == jnp.arange(slots, dtype=jnp.int32)[:, None]) & (on_path[None, :] > 0.5)
    ).astype(jnp.bfloat16)

    allowed = jnp.pad(
        allowed.reshape(every_row, n, owned), ((0, 0), (0, 0), (0, tree_rows - owned))
    ).reshape(every_row, n * tree_rows)
    any_space = pl.BlockSpec(memory_space=pl.ANY)
    in_vmem = pl.BlockSpec(memory_space=pltpu.VMEM)
    expand = pick.reshape(slots, n, owned, 1)[None] * jnp.eye(
        part_heads, dtype=jnp.bfloat16
    ).reshape(part_heads, 1, 1, 1, part_heads)
    expand = jnp.pad(
        expand.reshape(part_heads, slots, n, owned * part_heads),
        ((0, 0), (0, 0), (0, 0), (0, embed_rows - owned * part_heads)),
    ).reshape(part_heads, slots, n * embed_rows)
    num, stat, joined = pl.pallas_call(
        functools.partial(attention_kernel, n, q_rows, tree_rows),
        out_shape=[
            jax.ShapeDtypeStruct((every_row * GROUP, HEAD_WIDTH), jnp.float32),
            jax.ShapeDtypeStruct((every_row * GROUP, HEAD_WIDTH), jnp.float32),
            jax.ShapeDtypeStruct((slots, fc_embed.shape[1]), jnp.float32),
        ],
        in_specs=[any_space] * 3 + [in_vmem] * 2 + [any_space],
        out_specs=[in_vmem] * 3,
        scratch_shapes=[
            pltpu.VMEM(small.shape, jnp.bfloat16),
            pltpu.VMEM(fc_embed.shape, jnp.bfloat16),
            pltpu.VMEM((KEY_HEADS, positions, HEAD_WIDTH), jnp.bfloat16),
            pltpu.VMEM((KEY_HEADS, positions, HEAD_WIDTH), jnp.bfloat16),
            pltpu.VMEM((n * tree_rows, HEAD_WIDTH), jnp.bfloat16),
            pltpu.VMEM((n * tree_rows, HEAD_WIDTH), jnp.bfloat16),
            pltpu.VMEM((every_row * GROUP, 1), jnp.float32),
            pltpu.VMEM((every_row * GROUP, 1), jnp.float32),
            pltpu.SemaphoreType.DMA((n,)),
            pltpu.SemaphoreType.DMA((n,)),
            pltpu.SemaphoreType.DMA((2, KEY_HEADS)),
            pltpu.SemaphoreType.DMA((2, KEY_HEADS)),
            pltpu.SemaphoreType.DMA((4,)),
        ],
        compiler_params=pltpu.CompilerParams(
            collective_id=0, has_side_effects=True, vmem_limit_bytes=40 * 1024 * 1024
        ),
        cost_estimate=pl.CostEstimate(
            flops=4 * every_row * GROUP * positions * KEY_HEADS * HEAD_WIDTH,
            bytes_accessed=4 * prefix_key_heads.size,
            transcendentals=every_row * GROUP * positions * KEY_HEADS,
        ),
    )(small, prefix_key_heads, prefix_value_heads, allowed, expand, fc_embed)
    both = jnp.concatenate([num, stat], axis=1).reshape(
        every_row, members, part_heads, 2 * HEAD_WIDTH
    )
    both = lax.all_to_all(
        both.transpose(1, 0, 2, 3), "ctx", 0, 0, axis_index_groups=beside, tiled=True
    )
    num = both[..., :HEAD_WIDTH]
    top = both[..., HEAD_WIDTH]
    den = both[..., 2 * HEAD_WIDTH - 1]
    factor = jnp.exp(top - jnp.max(top, axis=0)[None])
    num = jnp.sum(num * factor[..., None], axis=0)
    den = jnp.sum(den * factor, axis=0)
    part = (num / den[..., None]).reshape(every_row, own_cols).astype(jnp.bfloat16)
    parts = jnp.pad(
        part.reshape(n, owned * part_heads, HEAD_WIDTH),
        ((0, 0), (0, embed_rows - owned * part_heads), (0, 0)),
    )

    def compact(x):
        return jnp.dot(pick, x, preferred_element_type=jnp.float32).astype(jnp.bfloat16)

    joined = joined + jnp.dot(compact(part), fc_feature, preferred_element_type=jnp.float32)
    own_pick = lax.dynamic_slice_in_dim(pick, me * owned, owned, 1).T.astype(jnp.float32)
    lanes = (joined.shape[1] // HEAD_WIDTH, HEAD_WIDTH)
    draft, arrived = pl.pallas_call(
        functools.partial(join_kernel, n),
        out_shape=[
            jax.ShapeDtypeStruct((owned,) + lanes, jnp.bfloat16),
            jax.ShapeDtypeStruct(parts.shape, jnp.bfloat16),
        ],
        in_specs=[pl.BlockSpec(memory_space=pltpu.SMEM)] + [in_vmem] * 3,
        out_specs=[in_vmem] * 2,
        scratch_shapes=[
            pltpu.VMEM((n,) + lanes, jnp.float32),
            pltpu.VMEM((slots,) + lanes, jnp.bfloat16),
            pltpu.VMEM(parts.shape, jnp.bfloat16),
        ]
        + [pltpu.SemaphoreType.DMA((n,))] * 6,
        compiler_params=pltpu.CompilerParams(
            collective_id=1, has_side_effects=True, vmem_limit_bytes=24 * 1024 * 1024
        ),
    )(own_pick, joined.reshape((slots,) + lanes), draft_gain.reshape(lanes), parts)
    draft_input = draft.reshape(owned, -1)
    attended = arrived[:, : owned * part_heads].reshape(n, owned, own_cols)
    attended = attended.transpose(1, 0, 2).reshape(owned, -1)
    return (attended, draft_input)


def solution(mesh):
    placed = (
        P(("groups", "ctx"), None),
        P(("groups", "ctx"), None),
        P(("groups", "ctx"), None),
        P(("groups", "ctx"), None),
        P(("groups", "ctx"), None),
        P(("groups", "ctx"), None),
        P("ctx", None),
        P("ctx", None),
        P(),
        P("groups", None),
        P("groups"),
    )
    return jax.shard_map(
        body,
        mesh=mesh,
        in_specs=placed,
        out_specs=(P(("groups", "ctx"), None), P(("groups", "ctx"), None)),
        check_vma=False,
    )
```
